32 devices in a mesh: cfg: 1, node: 32 (over z, y, x, core), pair: 1.
Axes of the slice: x: 2, y: 2, z: 4, core: 2. Of those that a mesh axis runs over, the one named last changes fastest.
Arguments:
- node_blocks: float32 [256, 2, 256, 256], P(('cfg', 'node'), None, None, 'pair'), may hold values from -1.5 to 1.5
- node_slot: int32 [256], replicated, may hold values from 0 to 255, as said below
- pair_list: int32 [128, 2], replicated, may hold values from 0 to 255, as said below
- second_list: int32 [128, 2], replicated, may hold values from 0 to 127, as said below
- targets: int32 [128], replicated, may hold values from 0 to 63, as said below
- spin_signs: int32 [128], replicated, may hold values from -1 to 1, as said below
Outputs:
- results: float32 [64, 2, 256, 256], P(('cfg', 'node'), None, None, 'pair')
The draws below stay inside these ranges and needn't reach their ends.
Inputs may be any that keep to these rules, and one draw needn't show every extreme that they name: `node_slot`: A permutation of the slots. `pair_list`: rows b * 4 to (b + 1) * 4 - 1 form block b. The first node of a pair in block b sits at a slot of b * 8 to (b + 1) * 8 - 1. For every block b and every owner o, at most 1 pair of block b has its second node at slots o * 8 to (o + 1) * 8 - 1; one owner supplies exactly 1 such node to every block. `second_list`: rows b * 4 to (b + 1) * 4 - 1 form block b. The first pair of a product in block b lies in block b of the pairs. For every block b and owner o, at most 1 product of block b has its second pair in block o of the pairs; one owner supplies exactly 1 such pair product to every block. `targets`: products of block b target results b * 2 to (b + 1) * 2 - 1. `spin_signs`: each entry is -1 or 1.
All inputs are finite; a program needn't handle non-finite values.
Results may differ from the reference program's by a relative error of at most 0.000098.
Values sent between devices are 32-bit elements; how exact they have to be, the bound alone decides.
A program may use at most 128 MiB of HBM per device.

```python
import jax
import jax.numpy as jnp
from jax import lax

ORDER = 256
NODE_COL = 8
PAIR_COL = 4
RES_COL = 2
CAP = 1
NODES = 256
PAIRS = 128
SECONDS = 128
RESULTS = 64


def owner_table(seed_key, columns):
    common_owner = jax.random.randint(jax.random.fold_in(seed_key, 0), (), 0, columns)

    def one_column(column):
        return jax.random.permutation(jax.random.fold_in(seed_key, column + 1), columns)
    orders = jax.vmap(one_column)(jnp.arange(columns))
    position = jnp.argmax((orders == common_owner).astype(jnp.int32), axis=1)
    leading = orders[:, 0]
    row_ids = jnp.arange(columns)
    orders = orders.at[row_ids, position].set(leading)
    orders = orders.at[:, 0].set(common_owner)
    return orders.astype(jnp.int32)


def contraction_graph(key):
    columns = NODES // NODE_COL
    node_slot = jax.random.permutation(jax.random.fold_in(key, 101), NODES).astype(jnp.int32)
    slot_node = jnp.argsort(node_slot).astype(jnp.int32)
    groups = jnp.arange(PAIR_COL) // CAP
    column_ids = jnp.arange(columns)[:, None]
    first_slot = column_ids * NODE_COL + jax.random.randint(jax.random.fold_in(key, 102), (columns, PAIR_COL), 0, NODE_COL)
    second_owner = owner_table(jax.random.fold_in(key, 103), columns)[:, groups]
    second_slot = second_owner * NODE_COL + jax.random.randint(jax.random.fold_in(key, 104), (columns, PAIR_COL), 0, NODE_COL)
    pair_list = jnp.stack([slot_node[first_slot], slot_node[second_slot]], axis=-1).reshape(PAIRS, 2)
    left_pair = column_ids * PAIR_COL + jax.random.randint(jax.random.fold_in(key, 105), (columns, PAIR_COL), 0, PAIR_COL)
    right_owner = owner_table(jax.random.fold_in(key, 106), columns)[:, groups]
    right_pair = right_owner * PAIR_COL + jax.random.randint(jax.random.fold_in(key, 107), (columns, PAIR_COL), 0, PAIR_COL)
    second_list = jnp.stack([left_pair, right_pair], axis=-1).reshape(SECONDS, 2)
    targets = (column_ids * RES_COL + jax.random.randint(jax.random.fold_in(key, 108), (columns, PAIR_COL), 0, RES_COL)).reshape(SECONDS)
    return (node_slot, pair_list.astype(jnp.int32), second_list.astype(jnp.int32), targets.astype(jnp.int32))


def draw_node_slot(key, part):
    return contraction_graph(key)[0]


def draw_pair_list(key, part):
    return contraction_graph(key)[1]


def draw_second_list(key, part):
    return contraction_graph(key)[2]


def draw_targets(key, part):
    return contraction_graph(key)[3]


def draw_spin_signs(key, part):
    return (2 * jax.random.randint(jax.random.fold_in(key, 201), (SECONDS,), 0, 2) - 1).astype(jnp.int32)


def level_of(key, extent, shards, low, top_value):
    def one(dim, shards_of):
        steps = jax.random.uniform(jax.random.fold_in(jax.random.fold_in(key, 6), dim), (shards_of,), jnp.float32, low / len(shards), top_value / len(shards))
        return jnp.repeat(jnp.exp(steps), extent[dim] // shards_of).reshape((-1,) + (1,) * (len(extent) - dim - 1))

    factor_of = one(*shards[0])
    for cut in shards[1:]:
        factor_of = factor_of * one(*cut)
    return factor_of


def gaussian(rng, dims, scale, bound, shards=(), kind=jnp.bfloat16):
    factor_of = level_of(rng, dims, shards, -0.22, 0.18) if shards else 1.0
    drawn = jax.random.normal(rng, dims, jnp.float32) * scale * factor_of
    return jnp.minimum(jnp.maximum(drawn, -bound), bound).astype(kind)


def setup_inputs(seed: int = 0, part: int = 0) -> dict:
    keys = jax.random.split(jax.random.key(seed), 7)
    part_keys = jax.random.split(jax.random.fold_in(keys[6], part), 7)
    node_blocks = gaussian(part_keys[0], (NODES, 2, ORDER, ORDER), ((2 * ORDER) ** -0.375), 1.5, ((0, 32),), jnp.float32)
    node_slot = draw_node_slot(jax.random.fold_in(keys[6], 71), part)
    pair_list = draw_pair_list(jax.random.fold_in(keys[6], 71), part)
    second_list = draw_second_list(jax.random.fold_in(keys[6], 71), part)
    targets = draw_targets(jax.random.fold_in(keys[6], 71), part)
    spin_signs = draw_spin_signs(jax.random.fold_in(keys[6], 71), part)
    return dict(node_blocks=node_blocks, node_slot=node_slot, pair_list=pair_list, second_list=second_list, targets=targets, spin_signs=spin_signs)


def matmul_high(left_side, right_side):
    return jnp.matmul(left_side, right_side, precision=lax.Precision.HIGHEST)


def complex_product(left_side, right_side):
    real_part = matmul_high(left_side[:, 0], right_side[:, 0]) - matmul_high(left_side[:, 1], right_side[:, 1])
    imag_part = matmul_high(left_side[:, 0], right_side[:, 1]) + matmul_high(left_side[:, 1], right_side[:, 0])
    return jnp.stack([real_part, imag_part], axis=1)


def reference(node_blocks, node_slot, pair_list, second_list, targets, spin_signs):
    first_nodes = jnp.take(node_blocks, node_slot[pair_list[:, 0]], axis=0)
    second_nodes = jnp.take(node_blocks, node_slot[pair_list[:, 1]], axis=0)
    products = complex_product(first_nodes, second_nodes)
    left_side = jnp.take(products, second_list[:, 0], axis=0)
    right_side = jnp.take(products, second_list[:, 1], axis=0)
    weights = spin_signs.astype(jnp.float32)[:, None, None, None]
    seconds = complex_product(left_side, right_side) * weights
    return jax.ops.segment_sum(seconds, targets, num_segments=RESULTS)
```

```python
import math

import jax
import jax.numpy as jnp
from jax import lax
from jax.sharding import PartitionSpec as P

GROUP = 8
STEPS = (8, 9, 10, 12)
RES_COL = 2


def complex_product(left_side, right_side):
    half_width = right_side.shape[3]
    stacked_left = jnp.concatenate([left_side[:, 0], left_side[:, 1]], axis=2)
    real_right = jnp.concatenate([right_side[:, 0], -right_side[:, 1]], axis=1)
    imag_right = jnp.concatenate([right_side[:, 1], right_side[:, 0]], axis=1)
    stacked_right = jnp.concatenate([real_right, imag_right], axis=2)
    joined = jnp.einsum(
        "jmk,jkn->jmn",
        stacked_left,
        stacked_right,
        precision=lax.Precision.HIGH,
        preferred_element_type=jnp.float32,
    )
    return jnp.stack([joined[:, :, :half_width], joined[:, :, half_width:]], axis=1)


def fetch(items, wanted, columns, column):
    count, _, rows, width = items.shape
    picks = wanted.shape[1]
    lanes = math.gcd(GROUP, columns)
    planes = columns // lanes
    plane, lane = column // lanes, column % lanes
    part = rows // lanes
    in_plane = [[p * lanes + q for q in range(lanes)] for p in range(planes)]
    in_line = [[p * lanes + q for p in range(planes)] for q in range(lanes)]
    held = lanes * count
    share = -(-count // planes)

    owners = wanted // count
    supplied = jnp.sum((owners.reshape(-1)[:, None] == jnp.arange(columns)[None, :]).astype(jnp.int32), axis=0)
    common = jnp.argmax(supplied).astype(jnp.int32)
    common_plane, common_lane = common // lanes, common % lanes
    is_common = owners == common

    flat = jnp.where(is_common, -1, wanted).reshape(planes, lanes * picks)
    need = jnp.any(flat[:, :, None] == jnp.arange(planes * held)[None, None, :], axis=1)
    need = need.reshape(planes, planes, held).transpose(1, 2, 0)
    foreign = jnp.arange(planes)[:, None] != jnp.arange(planes)[None, :]
    need = need & foreign[:, None, :]
    counted = need.astype(jnp.int32)
    lower = (jnp.arange(held)[:, None] > jnp.arange(held)[None, :]).astype(jnp.int32)
    rank = jnp.sum(lower[None, :, :, None] * counted[:, None, :, :], axis=2)
    most = jnp.max(jnp.sum(counted, axis=1))

    cut = items.reshape(count, 2, lanes, part, width).transpose(2, 0, 1, 3, 4)
    pieces = lax.all_to_all(cut, "node", 0, 0, axis_index_groups=in_plane, tiled=True)
    pieces = pieces.reshape(held, 2, part, width)

    mine = lax.dynamic_index_in_dim(counted, plane, 0, keepdims=False)
    my_rank = lax.dynamic_index_in_dim(rank, plane, 0, keepdims=False)
    to_me = lax.dynamic_index_in_dim(rank, plane, 2, keepdims=False)
    asked = lax.dynamic_slice_in_dim(wanted, plane * lanes, lanes, 0)
    asked_plane, asked_item = asked // held, asked % held
    asked_common = (asked // count) == common
    asked_rank = to_me[asked_plane, asked_item]
    shares = jnp.minimum(jnp.arange(planes * share), count - 1).reshape(planes, share)

    def across(capacity):
        def run(pieces):
            chosen = mine[:, :, None] * (my_rank[:, :, None] == jnp.arange(capacity)).astype(jnp.int32)
            listed = jnp.sum(chosen * jnp.arange(held)[:, None, None], axis=0)
            listed = jnp.concatenate([listed, common_lane * count + shares], axis=1)
            size = capacity + share
            packed = jnp.take(pieces, listed.reshape(-1), axis=0).reshape(planes, size, 2, part, width)
            came = lax.all_to_all(packed, "node", 0, 0, axis_index_groups=in_line, tiled=True)
            own_share = lax.dynamic_index_in_dim(came, common_plane, 0, keepdims=False)[capacity:]
            all_common = lax.all_gather(own_share, "node", axis=0, axis_index_groups=in_line, tiled=True)
            store = jnp.concatenate([pieces, came.reshape(planes * size, 2, part, width), all_common], axis=0)
            at = jnp.where(asked_plane == plane, asked_item, held + asked_plane * size + asked_rank)
            at = jnp.where(asked_common, held + planes * size + asked % count, at)
            return jnp.take(store, at.reshape(-1), axis=0)

        return run

    capacities = [c for c in STEPS if c < min(held, lanes * picks)] + [min(held, lanes * picks)]
    branch = jnp.sum((most > jnp.array(capacities[:-1], jnp.int32)).astype(jnp.int32))
    outgoing = lax.switch(branch, [across(c) for c in capacities], pieces)
    outgoing = outgoing.reshape(lanes, picks, 2, part, width)
    arrived = lax.all_to_all(outgoing, "node", 0, 0, axis_index_groups=in_plane, tiled=True)
    return arrived.transpose(1, 2, 0, 3, 4).reshape(picks, 2, rows, width)


def per_device(node_blocks, node_slot, pair_list, second_list, targets, spin_signs):
    columns = lax.axis_size("node")
    column = lax.axis_index("node")
    node_col = node_blocks.shape[0]
    pair_col = pair_list.shape[0] // columns
    block_start = column * pair_col
    own_pairs = lax.dynamic_slice_in_dim(pair_list, block_start, pair_col, 0)
    first_slot = node_slot[own_pairs[:, 0]] - column * node_col
    whole_nodes = lax.all_gather(node_blocks, "pair", axis=3, tiled=True)
    first_nodes = jnp.take(whole_nodes, first_slot, axis=0)
    wanted = node_slot[pair_list[:, 1]].reshape(columns, pair_col)
    second_nodes = fetch(node_blocks, wanted, columns, column)
    products = complex_product(first_nodes, second_nodes)
    whole_products = lax.all_gather(products, "pair", axis=3, tiled=True)
    own_seconds = lax.dynamic_slice_in_dim(second_list, block_start, pair_col, 0)
    left_side = jnp.take(whole_products, own_seconds[:, 0] - block_start, axis=0)
    right_side = fetch(products, second_list[:, 1].reshape(columns, pair_col), columns, column)
    own_signs = lax.dynamic_slice_in_dim(spin_signs, block_start, pair_col, 0).astype(jnp.float32)
    seconds = complex_product(left_side, right_side) * own_signs[:, None, None, None]
    return seconds, column


def solution(mesh):
    placed = (P(("cfg", "node"), None, None, "pair"), P(), P(), P(), P(), P())

    def run(node_blocks, node_slot, pair_list, second_list, targets, spin_signs):
        res_col = RES_COL

        def body(*args):
            seconds, column = per_device(*args)
            pair_col = seconds.shape[0]
            own = lax.dynamic_slice_in_dim(args[4], column * pair_col, pair_col, 0) - column * res_col
            return jnp.stack(
                [
                    jnp.sum(jnp.where((own == r)[:, None, None, None], seconds, 0.0), axis=0)
                    for r in range(res_col)
                ]
            )

        return jax.shard_map(
            body, mesh=mesh, in_specs=placed, out_specs=P(("cfg", "node"), None, None, "pair"), check_vma=False
        )(node_blocks, node_slot, pair_list, second_list, targets, spin_signs)

    return run
```

```python
import functools
import math

import jax
import jax.numpy as jnp
from jax import lax
from jax.experimental import pallas as pl
from jax.experimental.pallas import tpu as pltpu
from jax.sharding import PartitionSpec as P

GROUP = 8
STEPS = (9, 12)
CHUNKS = 4
MESH = pl.DeviceIdType.MESH
RES_COL = 2


def complex_product(left_side, right_side):
    half_width = right_side.shape[3]
    stacked_left = jnp.concatenate([left_side[:, 0], left_side[:, 1]], axis=2)
    real_right = jnp.concatenate([right_side[:, 0], -right_side[:, 1]], axis=1)
    imag_right = jnp.concatenate([right_side[:, 1], right_side[:, 0]], axis=1)
    stacked_right = jnp.concatenate([real_right, imag_right], axis=2)
    joined = jnp.einsum(
        "jmk,jkn->jmn",
        stacked_left,
        stacked_right,
        precision=lax.Precision.HIGH,
        preferred_element_type=jnp.float32,
    )
    return jnp.stack([joined[:, :, :half_width], joined[:, :, half_width:]], axis=1)


def exchange_kernel(
    lanes, planes, count, picks, capacity, share, chunks,
    send_table, hot_table, kind_table, place_table, items, out, *scratch,
):
    pieces, came, hot = scratch[:chunks], scratch[chunks : 2 * chunks], scratch[2 * chunks : 3 * chunks]
    packed, outgoing, s1, r1, s2, r2, s3, r3, s4, r4, own1, own4 = scratch[3 * chunks :]
    column = lax.axis_index("node")
    plane, lane = column // lanes, column % lanes
    rows = items.shape[2]
    part = rows // lanes
    step = part // chunks
    size = capacity + share

    def beside(e):
        return {"node": plane * lanes + lax.rem(lane + e, lanes)}

    def along(d):
        return {"node": lax.rem(plane + d, planes) * lanes + lane}

    barrier = pltpu.get_barrier_semaphore()
    for e in range(1, lanes):
        pl.semaphore_signal(barrier, inc=1, device_id=beside(e), device_id_type=MESH)
    for d in range(1, planes):
        pl.semaphore_signal(barrier, inc=1, device_id=along(d), device_id_type=MESH)
    pl.semaphore_wait(barrier, lanes - 1 + planes - 1)

    def rows_of(owner, c):
        return pl.ds(pl.multiple_of(owner * part + c * step, step), step)

    first = []
    for c in range(chunks):
        group = []
        for e in range(1, lanes):
            copy = pltpu.make_async_remote_copy(
                src_ref=items.at[:, :, rows_of(lax.rem(lane + e, lanes), c), :],
                dst_ref=pieces[c].at[pl.ds(lane * count, count)],
                send_sem=s1.at[c, e - 1], recv_sem=r1.at[c, e - 1],
                device_id=beside(e), device_id_type=MESH,
            )
            copy.start()
            group.append(copy)
        copy = pltpu.make_async_copy(
            items.at[:, :, rows_of(lane, c), :], pieces[c].at[pl.ds(lane * count, count)], own1.at[c]
        )
        copy.start()
        first.append((group, copy))

    second = []
    for c in range(chunks):
        group, own = first[c]
        for copy in group:
            copy.wait_recv()
        own.wait()
        sent = []
        for d in range(1, planes):
            target = lax.rem(plane + d, planes)

            def pack(k, carry, c=c, d=d, target=target):
                packed[c, d - 1, k] = pieces[c][send_table[target, k]]
                return carry

            lax.fori_loop(0, size, pack, 0)
            copy = pltpu.make_async_remote_copy(
                src_ref=packed.at[c, d - 1],
                dst_ref=came[c].at[pl.ds((d - 1) * size, size)],
                send_sem=s2.at[c, d - 1], recv_sem=r2.at[c, d - 1],
                device_id=along(d), device_id_type=MESH,
            )
            copy.start()
            sent.append(copy)
        second.append(sent)

    third = []
    for c in range(chunks):
        for copy in second[c]:
            copy.wait_recv()
        for i in range(share):
            here = pieces[c][hot_table[0, i]]
            there = came[c][hot_table[1, i]]
            local = hot_table[2, i]
            hot[c][plane * share + i] = jnp.where(local == 1, here, there)
        sent = []
        for d in range(1, planes):
            copy = pltpu.make_async_remote_copy(
                src_ref=hot[c].at[pl.ds(plane * share, share)],
                dst_ref=hot[c].at[pl.ds(plane * share, share)],
                send_sem=s3.at[c, d - 1], recv_sem=r3.at[c, d - 1],
                device_id=along(d), device_id_type=MESH,
            )
            copy.start()
            sent.append(copy)
        third.append(sent)

    last = []
    for c in range(chunks):
        for copy in third[c]:
            copy.wait_recv()
        sent = []
        for e in range(lanes):
            target = lax.rem(lane + e, lanes)
            for j in range(picks):
                kind, place = kind_table[target, j], place_table[target, j]
                a = pieces[c][jnp.where(kind == 0, place, 0)]
                b = came[c][jnp.where(kind == 1, place, 0)]
                h = hot[c][jnp.where(kind == 2, place, 0)]
                outgoing[c, e, j] = jnp.where(kind == 0, a, jnp.where(kind == 1, b, h))
            if e == 0:
                own = pltpu.make_async_copy(outgoing.at[c, e], out.at[:, :, rows_of(lane, c), :], own4.at[c])
                own.start()
                continue
            copy = pltpu.make_async_remote_copy(
                src_ref=outgoing.at[c, e],
                dst_ref=out.at[:, :, rows_of(lane, c), :],
                send_sem=s4.at[c, e - 1], recv_sem=r4.at[c, e - 1],
                device_id=beside(e), device_id_type=MESH,
            )
            copy.start()
            sent.append(copy)
        last.append((sent, own))

    for c in range(chunks):
        for copy in first[c][0] + second[c] + third[c]:
            copy.wait_send()
        for copy in last[c][0]:
            copy.wait()
        last[c][1].wait()


def exchange(lanes, planes, picks, capacity, share, collective_id, tables, items):
    count, _, rows, width = items.shape
    part = rows // lanes
    chunks = CHUNKS if part % (8 * CHUNKS) == 0 else 1
    step = part // chunks
    size = capacity + share
    block = (2, step, width)
    smem = pl.BlockSpec(memory_space=pltpu.SMEM)
    sems = [(chunks, n) for n in (lanes - 1, lanes - 1, planes - 1, planes - 1, planes - 1, planes - 1, lanes - 1, lanes - 1)]
    return pl.pallas_call(
        functools.partial(exchange_kernel, lanes, planes, count, picks, capacity, share, chunks),
        out_shape=jax.ShapeDtypeStruct((picks, 2, rows, width), jnp.float32),
        in_specs=[smem] * 4 + [pl.BlockSpec(memory_space=pl.ANY)],
        out_specs=pl.BlockSpec(memory_space=pl.ANY),
        scratch_shapes=[pltpu.VMEM((lanes * count, *block), jnp.float32)] * chunks
        + [pltpu.VMEM(((planes - 1) * size, *block), jnp.float32)] * chunks
        + [pltpu.VMEM((planes * share, *block), jnp.float32)] * chunks
        + [pltpu.VMEM((chunks, planes - 1, size, *block), jnp.float32)]
        + [pltpu.VMEM((chunks, lanes, picks, *block), jnp.float32)]
        + [pltpu.SemaphoreType.DMA(s) for s in sems]
        + [pltpu.SemaphoreType.DMA((chunks,))] * 2,
        compiler_params=pltpu.CompilerParams(
            collective_id=collective_id, has_side_effects=True, vmem_limit_bytes=40 * 2**20
        ),
    )(*tables, items)


def fetch(items, wanted, columns, column, first_id):
    count, _, rows, width = items.shape
    picks = wanted.shape[1]
    lanes = math.gcd(GROUP, columns)
    planes = columns // lanes
    plane, lane = column // lanes, column % lanes
    part = rows // lanes
    in_plane = [[p * lanes + q for q in range(lanes)] for p in range(planes)]
    in_line = [[p * lanes + q for p in range(planes)] for q in range(lanes)]
    held = lanes * count
    share = -(-count // planes)

    owners = wanted // count
    supplied = jnp.sum((owners.reshape(-1)[:, None] == jnp.arange(columns)[None, :]).astype(jnp.int32), axis=0)
    common = jnp.argmax(supplied).astype(jnp.int32)
    common_plane, common_lane = common // lanes, common % lanes
    is_common = owners == common

    flat = jnp.where(is_common, -1, wanted).reshape(planes, lanes * picks)
    need = jnp.any(flat[:, :, None] == jnp.arange(planes * held)[None, None, :], axis=1)
    need = need.reshape(planes, planes, held).transpose(1, 2, 0)
    foreign = jnp.arange(planes)[:, None] != jnp.arange(planes)[None, :]
    need = need & foreign[:, None, :]
    counted = need.astype(jnp.int32)
    lower = (jnp.arange(held)[:, None] > jnp.arange(held)[None, :]).astype(jnp.int32)
    rank = jnp.sum(lower[None, :, :, None] * counted[:, None, :, :], axis=2)
    most = jnp.max(jnp.sum(counted, axis=1))

    mine = lax.dynamic_index_in_dim(counted, plane, 0, keepdims=False)
    my_rank = lax.dynamic_index_in_dim(rank, plane, 0, keepdims=False)
    to_me = lax.dynamic_index_in_dim(rank, plane, 2, keepdims=False)
    asked = lax.dynamic_slice_in_dim(wanted, plane * lanes, lanes, 0)
    asked_plane, asked_item = asked // held, asked % held
    asked_common = (asked // count) == common
    asked_rank = to_me[asked_plane, asked_item]
    shares = jnp.minimum(jnp.arange(planes * share), count - 1).reshape(planes, share)

    def listing(capacity):
        chosen = mine[:, :, None] * (my_rank[:, :, None] == jnp.arange(capacity)).astype(jnp.int32)
        listed = jnp.sum(chosen * jnp.arange(held)[:, None, None], axis=0)
        return jnp.concatenate([listed, common_lane * count + shares], axis=1)

    def general(capacity):
        def run(items):
            cut = items.reshape(count, 2, lanes, part, width).transpose(2, 0, 1, 3, 4)
            pieces = lax.all_to_all(cut, "node", 0, 0, axis_index_groups=in_plane, tiled=True)
            pieces = pieces.reshape(held, 2, part, width)
            listed = listing(capacity)
            size = capacity + share
            packed = jnp.take(pieces, listed.reshape(-1), axis=0).reshape(planes, size, 2, part, width)
            came = lax.all_to_all(packed, "node", 0, 0, axis_index_groups=in_line, tiled=True)
            own_share = lax.dynamic_index_in_dim(came, common_plane, 0, keepdims=False)[capacity:]
            all_common = lax.all_gather(own_share, "node", axis=0, axis_index_groups=in_line, tiled=True)
            store = jnp.concatenate([pieces, came.reshape(planes * size, 2, part, width), all_common], axis=0)
            at = jnp.where(asked_plane == plane, asked_item, held + asked_plane * size + asked_rank)
            at = jnp.where(asked_common, held + planes * size + asked % count, at)
            outgoing = jnp.take(store, at.reshape(-1), axis=0).reshape(lanes, picks, 2, part, width)
            arrived = lax.all_to_all(outgoing, "node", 0, 0, axis_index_groups=in_plane, tiled=True)
            return arrived.transpose(1, 2, 0, 3, 4).reshape(picks, 2, rows, width)

        return run

    def direct(capacity, collective_id):
        size = capacity + share
        distance = lax.rem(plane - asked_plane + planes, planes)
        kind = jnp.where(asked_common, 2, jnp.where(distance == 0, 0, 1)).astype(jnp.int32)
        place = jnp.where(distance == 0, asked_item, (distance - 1) * size + asked_rank)
        place = jnp.where(asked_common, asked % count, place).astype(jnp.int32)
        away = lax.rem(plane - common_plane + planes, planes)
        here = common_lane * count + lax.dynamic_index_in_dim(shares, plane, 0, keepdims=False)
        there = jnp.maximum(away - 1, 0) * size + capacity + jnp.arange(share)
        local = jnp.broadcast_to((away == 0).astype(jnp.int32), (share,))
        hot_table = jnp.stack([here, there, local]).astype(jnp.int32)

        def run(items):
            tables = (listing(capacity).astype(jnp.int32), hot_table, kind, place)
            return exchange(lanes, planes, picks, capacity, share, collective_id, tables, items)

        return run

    limit = min(held, lanes * picks)
    steps = [c for c in STEPS if c < limit]
    branch = jnp.sum((most > jnp.array(steps, jnp.int32)).astype(jnp.int32))
    branches = [direct(c, first_id + i) for i, c in enumerate(steps)] + [general(limit)]
    return lax.switch(branch, branches, items)


def per_device(node_blocks, node_slot, pair_list, second_list, targets, spin_signs):
    columns = lax.axis_size("node")
    column = lax.axis_index("node")
    node_col = node_blocks.shape[0]
    pair_col = pair_list.shape[0] // columns
    block_start = column * pair_col
    own_pairs = lax.dynamic_slice_in_dim(pair_list, block_start, pair_col, 0)
    first_slot = node_slot[own_pairs[:, 0]] - column * node_col
    whole_nodes = lax.all_gather(node_blocks, "pair", axis=3, tiled=True)
    first_nodes = jnp.take(whole_nodes, first_slot, axis=0)
    wanted = node_slot[pair_list[:, 1]].reshape(columns, pair_col)
    second_nodes = fetch(node_blocks, wanted, columns, column, 0)
    products = complex_product(first_nodes, second_nodes)
    whole_products = lax.all_gather(products, "pair", axis=3, tiled=True)
    own_seconds = lax.dynamic_slice_in_dim(second_list, block_start, pair_col, 0)
    left_side = jnp.take(whole_products, own_seconds[:, 0] - block_start, axis=0)
    right_side = fetch(products, second_list[:, 1].reshape(columns, pair_col), columns, column, len(STEPS))
    own_signs = lax.dynamic_slice_in_dim(spin_signs, block_start, pair_col, 0).astype(jnp.float32)
    seconds = complex_product(left_side, right_side) * own_signs[:, None, None, None]
    return seconds, column


def solution(mesh):
    placed = (P(("cfg", "node"), None, None, "pair"), P(), P(), P(), P(), P())

    def run(node_blocks, node_slot, pair_list, second_list, targets, spin_signs):
        res_col = RES_COL

        def body(*args):
            seconds, column = per_device(*args)
            pair_col = seconds.shape[0]
            own = lax.dynamic_slice_in_dim(args[4], column * pair_col, pair_col, 0) - column * res_col
            return jnp.stack(
                [
                    jnp.sum(jnp.where((own == r)[:, None, None, None], seconds, 0.0), axis=0)
                    for r in range(res_col)
                ]
            )

        return jax.shard_map(
            body, mesh=mesh, in_specs=placed, out_specs=P(("cfg", "node"), None, None, "pair"), check_vma=False
        )(node_blocks, node_slot, pair_list, second_list, targets, spin_signs)

    return run
```

```python
import functools
import math

import jax
import jax.numpy as jnp
from jax import lax
from jax.experimental import pallas as pl
from jax.experimental.pallas import tpu as pltpu
from jax.sharding import PartitionSpec as P

GROUP = 8
STEPS = (8, 9, 11)
EXTRA = 3
CHUNKS = 4
MESH = pl.DeviceIdType.MESH
RES_COL = 2


def complex_product(left_side, right_side):
    half_width = right_side.shape[3]
    stacked_left = jnp.concatenate([left_side[:, 0], left_side[:, 1]], axis=2)
    real_right = jnp.concatenate([right_side[:, 0], -right_side[:, 1]], axis=1)
    imag_right = jnp.concatenate([right_side[:, 1], right_side[:, 0]], axis=1)
    stacked_right = jnp.concatenate([real_right, imag_right], axis=2)
    joined = jnp.einsum(
        "jmk,jkn->jmn",
        stacked_left,
        stacked_right,
        precision=lax.Precision.HIGH,
        preferred_element_type=jnp.float32,
    )
    return jnp.stack([joined[:, :, :half_width], joined[:, :, half_width:]], axis=1)


def exchange_kernel(
    lanes, planes, count, picks, capacity, share, chunks,
    send_table, hot_table, kind_table, place_table, items, out, *scratch,
):
    pieces, came, hot = scratch[:chunks], scratch[chunks : 2 * chunks], scratch[2 * chunks : 3 * chunks]
    packed, outgoing, s1, r1, s2, r2, s3, r3, s4, r4, own1, own4 = scratch[3 * chunks :]
    column = lax.axis_index("node")
    plane, lane = column // lanes, column % lanes
    rows = items.shape[2]
    part = rows // lanes
    step = part // chunks
    size = capacity + share

    def beside(e):
        return {"node": plane * lanes + lax.rem(lane + e, lanes)}

    def facing(d):
        low = (plane % 2) * 2
        high = ((plane // 2) % 2) * 4
        return plane + (1 - low if d % 2 else 0) + (2 - high if d >= 2 else 0)

    def along(d):
        return {"node": facing(d) * lanes + lane}

    def size_of(d):
        return size + (EXTRA if d == 1 else 0)

    def offset_of(d):
        return (d - 1) * size + (EXTRA if d > 1 else 0)

    barrier = pltpu.get_barrier_semaphore()
    for e in range(1, lanes):
        pl.semaphore_signal(barrier, inc=1, device_id=beside(e), device_id_type=MESH)
    for d in range(1, planes):
        pl.semaphore_signal(barrier, inc=1, device_id=along(d), device_id_type=MESH)
    pl.semaphore_wait(barrier, lanes - 1 + planes - 1)

    def rows_of(owner, c):
        return pl.ds(pl.multiple_of(owner * part + c * step, step), step)

    first, second, third, last = {}, {}, {}, {}

    def spread(c):
        group = []
        for e in range(1, lanes):
            copy = pltpu.make_async_remote_copy(
                src_ref=items.at[:, :, rows_of(lax.rem(lane + e, lanes), c), :],
                dst_ref=pieces[c].at[pl.ds(lane * count, count)],
                send_sem=s1.at[c, e - 1], recv_sem=r1.at[c, e - 1],
                device_id=beside(e), device_id_type=MESH,
            )
            copy.start()
            group.append(copy)
        copy = pltpu.make_async_copy(
            items.at[:, :, rows_of(lane, c), :], pieces[c].at[pl.ds(lane * count, count)], own1.at[c]
        )
        copy.start()
        first[c] = (group, copy)

    def gathered(c):
        for copy in first[c][0]:
            copy.wait_recv()
        first[c][1].wait()

    def pack(c):
        for d in range(1, planes):
            target = facing(d)

            def move(k, carry, d=d, target=target):
                packed[c, d - 1, k] = pieces[c][send_table[target, k]]
                return carry

            lax.fori_loop(0, size_of(d), move, 0)

    def cross(c):
        second[c] = []
        for d in range(1, planes):
            copy = pltpu.make_async_remote_copy(
                src_ref=packed.at[c, d - 1, pl.ds(0, size_of(d))],
                dst_ref=came[c].at[pl.ds(offset_of(d), size_of(d))],
                send_sem=s2.at[c, d - 1], recv_sem=r2.at[c, d - 1],
                device_id=along(d), device_id_type=MESH,
            )
            copy.start()
            second[c].append(copy)

    def crossed(c):
        for copy in second[c]:
            copy.wait_recv()

    def pass_on(c):
        for i in range(share):
            here = pieces[c][hot_table[0, i]]
            there = came[c][hot_table[1, i]]
            hot[c][plane * share + i] = jnp.where(hot_table[2, i] == 1, here, there)
        third[c] = []
        for d in range(1, planes):
            copy = pltpu.make_async_remote_copy(
                src_ref=hot[c].at[pl.ds(plane * share, share)],
                dst_ref=hot[c].at[pl.ds(plane * share, share)],
                send_sem=s3.at[c, d - 1], recv_sem=r3.at[c, d - 1],
                device_id=along(d), device_id_type=MESH,
            )
            copy.start()
            third[c].append(copy)

    def deliver(c):
        for copy in third[c]:
            copy.wait_recv()
        sent = []
        for e in range(lanes):
            target = lax.rem(lane + e, lanes)

            def move(j, carry, e=e, target=target):
                kind, place = kind_table[target, j], place_table[target, j]
                a = pieces[c][jnp.where(kind == 0, place, 0)]
                b = came[c][jnp.where(kind == 1, place, 0)]
                h = hot[c][jnp.where(kind == 2, place, 0)]
                outgoing[c, e, j] = jnp.where(kind == 0, a, jnp.where(kind == 1, b, h))
                return carry

            lax.fori_loop(0, picks, move, 0)
            if e == 0:
                own = pltpu.make_async_copy(outgoing.at[c, e], out.at[:, :, rows_of(lane, c), :], own4.at[c])
                own.start()
                continue
            copy = pltpu.make_async_remote_copy(
                src_ref=outgoing.at[c, e],
                dst_ref=out.at[:, :, rows_of(lane, c), :],
                send_sem=s4.at[c, e - 1], recv_sem=r4.at[c, e - 1],
                device_id=beside(e), device_id_type=MESH,
            )
            copy.start()
            sent.append(copy)
        last[c] = (sent, own)

    spread(0)
    for c in range(chunks):
        gathered(c)
        if c + 1 < chunks:
            spread(c + 1)
        pack(c)
        if c < 2:
            cross(c)
    for c in range(chunks):
        crossed(c)
        if c + 2 < chunks:
            cross(c + 2)
        pass_on(c)
        if c > 0:
            deliver(c - 1)
    deliver(chunks - 1)

    for c in range(chunks):
        for copy in first[c][0] + second[c] + third[c]:
            copy.wait_send()
        for copy in last[c][0]:
            copy.wait()
        last[c][1].wait()


def exchange(lanes, planes, picks, capacity, share, collective_id, tables, items):
    count, _, rows, width = items.shape
    part = rows // lanes
    chunks = CHUNKS if part % (8 * CHUNKS) == 0 else 1
    step = part // chunks
    size = capacity + share
    block = (2, step, width)
    smem = pl.BlockSpec(memory_space=pltpu.SMEM)
    sems = [(chunks, n) for n in (lanes - 1, lanes - 1, planes - 1, planes - 1, planes - 1, planes - 1, lanes - 1, lanes - 1)]
    return pl.pallas_call(
        functools.partial(exchange_kernel, lanes, planes, count, picks, capacity, share, chunks),
        out_shape=jax.ShapeDtypeStruct((picks, 2, rows, width), jnp.float32),
        in_specs=[smem] * 4 + [pl.BlockSpec(memory_space=pl.ANY)],
        out_specs=pl.BlockSpec(memory_space=pl.ANY),
        scratch_shapes=[pltpu.VMEM((lanes * count, *block), jnp.float32)] * chunks
        + [pltpu.VMEM(((planes - 1) * size + EXTRA, *block), jnp.float32)] * chunks
        + [pltpu.VMEM((planes * share, *block), jnp.float32)] * chunks
        + [pltpu.VMEM((chunks, planes - 1, size + EXTRA, *block), jnp.float32)]
        + [pltpu.VMEM((chunks, lanes, picks, *block), jnp.float32)]
        + [pltpu.SemaphoreType.DMA(s) for s in sems]
        + [pltpu.SemaphoreType.DMA((chunks,))] * 2,
        compiler_params=pltpu.CompilerParams(
            collective_id=collective_id, has_side_effects=True, vmem_limit_bytes=40 * 2**20
        ),
    )(*tables, items)


def fetch(items, wanted, columns, column, first_id):
    count, _, rows, width = items.shape
    picks = wanted.shape[1]
    lanes = math.gcd(GROUP, columns)
    planes = columns // lanes
    plane, lane = column // lanes, column % lanes
    part = rows // lanes
    in_plane = [[p * lanes + q for q in range(lanes)] for p in range(planes)]
    in_line = [[p * lanes + q for p in range(planes)] for q in range(lanes)]
    held = lanes * count
    share = -(-count // planes)

    owners = wanted // count
    supplied = jnp.sum((owners.reshape(-1)[:, None] == jnp.arange(columns)[None, :]).astype(jnp.int32), axis=0)
    common = jnp.argmax(supplied).astype(jnp.int32)
    common_plane, common_lane = common // lanes, common % lanes
    is_common = owners == common

    flat = jnp.where(is_common, -1, wanted).reshape(planes, lanes * picks)
    need = jnp.any(flat[:, :, None] == jnp.arange(planes * held)[None, None, :], axis=1)
    need = need.reshape(planes, planes, held).transpose(1, 2, 0)
    foreign = jnp.arange(planes)[:, None] != jnp.arange(planes)[None, :]
    need = need & foreign[:, None, :]
    counted = need.astype(jnp.int32)
    lower = (jnp.arange(held)[:, None] > jnp.arange(held)[None, :]).astype(jnp.int32)
    rank = jnp.sum(lower[None, :, :, None] * counted[:, None, :, :], axis=2)
    totals = jnp.sum(counted, axis=1)
    near = (jnp.arange(planes)[:, None] // 2) == (jnp.arange(planes)[None, :] // 2)
    most = jnp.max(totals - EXTRA * near.astype(jnp.int32))

    mine = lax.dynamic_index_in_dim(counted, plane, 0, keepdims=False)
    my_rank = lax.dynamic_index_in_dim(rank, plane, 0, keepdims=False)
    to_me = lax.dynamic_index_in_dim(rank, plane, 2, keepdims=False)
    asked = lax.dynamic_slice_in_dim(wanted, plane * lanes, lanes, 0)
    asked_plane, asked_item = asked // held, asked % held
    asked_common = (asked // count) == common
    asked_rank = to_me[asked_plane, asked_item]
    shares = jnp.minimum(jnp.arange(planes * share), count - 1).reshape(planes, share)

    def listing(capacity, first=False):
        chosen = mine[:, :, None] * (my_rank[:, :, None] == jnp.arange(capacity)).astype(jnp.int32)
        listed = jnp.sum(chosen * jnp.arange(held)[:, None, None], axis=0)
        parts = [common_lane * count + shares, listed]
        return jnp.concatenate(parts if first else parts[::-1], axis=1)

    def general(capacity):
        def run(items):
            cut = items.reshape(count, 2, lanes, part, width).transpose(2, 0, 1, 3, 4)
            pieces = lax.all_to_all(cut, "node", 0, 0, axis_index_groups=in_plane, tiled=True)
            pieces = pieces.reshape(held, 2, part, width)
            listed = listing(capacity)
            size = capacity + share
            packed = jnp.take(pieces, listed.reshape(-1), axis=0).reshape(planes, size, 2, part, width)
            came = lax.all_to_all(packed, "node", 0, 0, axis_index_groups=in_line, tiled=True)
            own_share = lax.dynamic_index_in_dim(came, common_plane, 0, keepdims=False)[capacity:]
            all_common = lax.all_gather(own_share, "node", axis=0, axis_index_groups=in_line, tiled=True)
            store = jnp.concatenate([pieces, came.reshape(planes * size, 2, part, width), all_common], axis=0)
            at = jnp.where(asked_plane == plane, asked_item, held + asked_plane * size + asked_rank)
            at = jnp.where(asked_common, held + planes * size + asked % count, at)
            outgoing = jnp.take(store, at.reshape(-1), axis=0).reshape(lanes, picks, 2, part, width)
            arrived = lax.all_to_all(outgoing, "node", 0, 0, axis_index_groups=in_plane, tiled=True)
            return arrived.transpose(1, 2, 0, 3, 4).reshape(picks, 2, rows, width)

        return run

    def direct(capacity, collective_id):
        size = capacity + share
        distance = plane ^ asked_plane

        def offset(d):
            return jnp.maximum((d - 1) * size + EXTRA * (d > 1), 0)

        kind = jnp.where(asked_common, 2, jnp.where(distance == 0, 0, 1)).astype(jnp.int32)
        place = jnp.where(distance == 0, asked_item, offset(distance) + share + asked_rank)
        place = jnp.where(asked_common, asked % count, place).astype(jnp.int32)
        away = plane ^ common_plane
        here = common_lane * count + lax.dynamic_index_in_dim(shares, plane, 0, keepdims=False)
        there = offset(away) + jnp.arange(share)
        local = jnp.broadcast_to((away == 0).astype(jnp.int32), (share,))
        hot_table = jnp.stack([here, there, local]).astype(jnp.int32)

        def run(items):
            tables = (listing(capacity + EXTRA, True).astype(jnp.int32), hot_table, kind, place)
            return exchange(lanes, planes, picks, capacity, share, collective_id, tables, items)

        return run

    limit = min(held, lanes * picks)
    steps = [c for c in STEPS if c + EXTRA < limit and planes == 4]
    if not steps:
        return general(limit)(items)
    branch = jnp.sum((most > jnp.array(steps, jnp.int32)).astype(jnp.int32))
    branches = [direct(c, first_id + i) for i, c in enumerate(steps)] + [general(limit)]
    return lax.switch(branch, branches, items)


def per_device(node_blocks, node_slot, pair_list, second_list, targets, spin_signs):
    columns = lax.axis_size("node")
    column = lax.axis_index("node")
    node_col = node_blocks.shape[0]
    pair_col = pair_list.shape[0] // columns
    block_start = column * pair_col
    own_pairs = lax.dynamic_slice_in_dim(pair_list, block_start, pair_col, 0)
    first_slot = node_slot[own_pairs[:, 0]] - column * node_col
    whole_nodes = lax.all_gather(node_blocks, "pair", axis=3, tiled=True)
    first_nodes = jnp.take(whole_nodes, first_slot, axis=0)
    wanted = node_slot[pair_list[:, 1]].reshape(columns, pair_col)
    second_nodes = fetch(node_blocks, wanted, columns, column, 0)
    products = complex_product(first_nodes, second_nodes)
    whole_products = lax.all_gather(products, "pair", axis=3, tiled=True)
    own_seconds = lax.dynamic_slice_in_dim(second_list, block_start, pair_col, 0)
    left_side = jnp.take(whole_products, own_seconds[:, 0] - block_start, axis=0)
    right_side = fetch(products, second_list[:, 1].reshape(columns, pair_col), columns, column, len(STEPS))
    own_signs = lax.dynamic_slice_in_dim(spin_signs, block_start, pair_col, 0).astype(jnp.float32)
    seconds = complex_product(left_side, right_side) * own_signs[:, None, None, None]
    return seconds, column


def solution(mesh):
    placed = (P(("cfg", "node"), None, None, "pair"), P(), P(), P(), P(), P())

    def run(node_blocks, node_slot, pair_list, second_list, targets, spin_signs):
        res_col = RES_COL

        def body(*args):
            seconds, column = per_device(*args)
            pair_col = seconds.shape[0]
            own = lax.dynamic_slice_in_dim(args[4], column * pair_col, pair_col, 0) - column * res_col
            return jnp.stack(
                [
                    jnp.sum(jnp.where((own == r)[:, None, None, None], seconds, 0.0), axis=0)
                    for r in range(res_col)
                ]
            )

        return jax.shard_map(
            body, mesh=mesh, in_specs=placed, out_specs=P(("cfg", "node"), None, None, "pair"), check_vma=False
        )(node_blocks, node_slot, pair_list, second_list, targets, spin_signs)

    return run
```

```python
import functools
import math

import jax
import jax.numpy as jnp
from jax import lax
from jax.experimental import pallas as pl
from jax.experimental.pallas import tpu as pltpu
from jax.sharding import PartitionSpec as P

GROUP = 8
STEPS = (8, 10)
EXTRA = 3
CHUNKS = 4
MESH = pl.DeviceIdType.MESH
RES_COL = 2


def complex_product(left_side, right_side):
    half_width = right_side.shape[3]
    stacked_left = jnp.concatenate([left_side[:, 0], left_side[:, 1]], axis=2)
    real_right = jnp.concatenate([right_side[:, 0], -right_side[:, 1]], axis=1)
    imag_right = jnp.concatenate([right_side[:, 1], right_side[:, 0]], axis=1)
    stacked_right = jnp.concatenate([real_right, imag_right], axis=2)
    joined = jnp.einsum(
        "jmk,jkn->jmn",
        stacked_left,
        stacked_right,
        precision=lax.Precision.HIGH,
        preferred_element_type=jnp.float32,
    )
    return jnp.stack([joined[:, :, :half_width], joined[:, :, half_width:]], axis=1)


def exchange_kernel(
    lanes, planes, count, picks, capacity, share, chunks,
    send_table, hot_table, kind_table, place_table, items, out, *scratch,
):
    pieces, came, hot = scratch[:chunks], scratch[chunks : 2 * chunks], scratch[2 * chunks : 3 * chunks]
    packed, outgoing, s1, r1, s2, r2, s3, r3, s4, r4, own1, own4 = scratch[3 * chunks :]
    column = lax.axis_index("node")
    plane, lane = column // lanes, column % lanes
    rows = items.shape[2]
    part = rows // lanes
    step = part // chunks
    size = capacity + share

    def beside(e):
        return {"node": plane * lanes + lax.rem(lane + e, lanes)}

    def facing(d):
        low = (plane % 2) * 2
        high = ((plane // 2) % 2) * 4
        return plane + (1 - low if d % 2 else 0) + (2 - high if d >= 2 else 0)

    def along(d):
        return {"node": facing(d) * lanes + lane}

    def size_of(d):
        return size + (EXTRA if d == 1 else 0)

    def offset_of(d):
        return (d - 1) * size + (EXTRA if d > 1 else 0)

    barrier = pltpu.get_barrier_semaphore()
    for e in range(1, lanes):
        pl.semaphore_signal(barrier, inc=1, device_id=beside(e), device_id_type=MESH)
    for d in range(1, planes):
        pl.semaphore_signal(barrier, inc=1, device_id=along(d), device_id_type=MESH)
    pl.semaphore_wait(barrier, lanes - 1 + planes - 1)

    def rows_of(owner, c):
        return pl.ds(pl.multiple_of(owner * part + c * step, step), step)

    first, second, third, last = {}, {}, {}, {}

    def spread(c):
        group = []
        for e in range(1, lanes):
            copy = pltpu.make_async_remote_copy(
                src_ref=items.at[:, :, rows_of(lax.rem(lane + e, lanes), c), :],
                dst_ref=pieces[c].at[pl.ds(lane * count, count)],
                send_sem=s1.at[c, e - 1], recv_sem=r1.at[c, e - 1],
                device_id=beside(e), device_id_type=MESH,
            )
            copy.start()
            group.append(copy)
        copy = pltpu.make_async_copy(
            items.at[:, :, rows_of(lane, c), :], pieces[c].at[pl.ds(lane * count, count)], own1.at[c]
        )
        copy.start()
        first[c] = (group, copy)

    def gathered(c):
        for copy in first[c][0]:
            copy.wait_recv()
        first[c][1].wait()

    def pack(c):
        for d in range(1, planes):
            target = facing(d)

            def move(k, carry, d=d, target=target):
                packed[c, d - 1, k] = pieces[c][send_table[target, k]]
                return carry

            lax.fori_loop(0, size_of(d), move, 0)

    def cross(c):
        second[c] = []
        for d in range(1, planes):
            copy = pltpu.make_async_remote_copy(
                src_ref=packed.at[c, d - 1, pl.ds(0, size_of(d))],
                dst_ref=came[c].at[pl.ds(offset_of(d), size_of(d))],
                send_sem=s2.at[c, d - 1], recv_sem=r2.at[c, d - 1],
                device_id=along(d), device_id_type=MESH,
            )
            copy.start()
            second[c].append(copy)

    def crossed(c):
        for copy in second[c]:
            copy.wait_recv()

    def pass_on(c):
        for i in range(share):
            here = pieces[c][hot_table[0, i]]
            there = came[c][hot_table[1, i]]
            hot[c][plane * share + i] = jnp.where(hot_table[2, i] == 1, here, there)
        third[c] = []
        for d in range(1, planes):
            copy = pltpu.make_async_remote_copy(
                src_ref=hot[c].at[pl.ds(plane * share, share)],
                dst_ref=hot[c].at[pl.ds(plane * share, share)],
                send_sem=s3.at[c, d - 1], recv_sem=r3.at[c, d - 1],
                device_id=along(d), device_id_type=MESH,
            )
            copy.start()
            third[c].append(copy)

    def deliver(c):
        for copy in third[c]:
            copy.wait_recv()
        sent = []
        for e in range(lanes):
            target = lax.rem(lane + e, lanes)

            def move(j, carry, e=e, target=target):
                kind, place = kind_table[target, j], place_table[target, j]
                a = pieces[c][jnp.where(kind == 0, place, 0)]
                b = came[c][jnp.where(kind == 1, place, 0)]
                h = hot[c][jnp.where(kind == 2, place, 0)]
                outgoing[c, e, j] = jnp.where(kind == 0, a, jnp.where(kind == 1, b, h))
                return carry

            lax.fori_loop(0, picks, move, 0)
            if e == 0:
                own = pltpu.make_async_copy(outgoing.at[c, e], out.at[:, :, rows_of(lane, c), :], own4.at[c])
                own.start()
                continue
            copy = pltpu.make_async_remote_copy(
                src_ref=outgoing.at[c, e],
                dst_ref=out.at[:, :, rows_of(lane, c), :],
                send_sem=s4.at[c, e - 1], recv_sem=r4.at[c, e - 1],
                device_id=beside(e), device_id_type=MESH,
            )
            copy.start()
            sent.append(copy)
        last[c] = (sent, own)

    spread(0)
    for c in range(chunks):
        gathered(c)
        if c + 1 < chunks:
            spread(c + 1)
        pack(c)
        cross(c)
    for c in range(chunks):
        crossed(c)
        pass_on(c)
        if c > 0:
            deliver(c - 1)
    deliver(chunks - 1)

    for c in range(chunks):
        for copy in first[c][0] + second[c] + third[c]:
            copy.wait_send()
        for copy in last[c][0]:
            copy.wait()
        last[c][1].wait()


def exchange(lanes, planes, picks, capacity, share, collective_id, tables, items):
    count, _, rows, width = items.shape
    part = rows // lanes
    chunks = CHUNKS if part % (8 * CHUNKS) == 0 else 1
    step = part // chunks
    size = capacity + share
    block = (2, step, width)
    smem = pl.BlockSpec(memory_space=pltpu.SMEM)
    sems = [(chunks, n) for n in (lanes - 1, lanes - 1, planes - 1, planes - 1, planes - 1, planes - 1, lanes - 1, lanes - 1)]
    return pl.pallas_call(
        functools.partial(exchange_kernel, lanes, planes, count, picks, capacity, share, chunks),
        out_shape=jax.ShapeDtypeStruct((picks, 2, rows, width), jnp.float32),
        in_specs=[smem] * 4 + [pl.BlockSpec(memory_space=pl.ANY)],
        out_specs=pl.BlockSpec(memory_space=pl.ANY),
        scratch_shapes=[pltpu.VMEM((lanes * count, *block), jnp.float32)] * chunks
        + [pltpu.VMEM(((planes - 1) * size + EXTRA, *block), jnp.float32)] * chunks
        + [pltpu.VMEM((planes * share, *block), jnp.float32)] * chunks
        + [pltpu.VMEM((chunks, planes - 1, size + EXTRA, *block), jnp.float32)]
        + [pltpu.VMEM((chunks, lanes, picks, *block), jnp.float32)]
        + [pltpu.SemaphoreType.DMA(s) for s in sems]
        + [pltpu.SemaphoreType.DMA((chunks,))] * 2,
        compiler_params=pltpu.CompilerParams(
            collective_id=collective_id, has_side_effects=True, vmem_limit_bytes=40 * 2**20
        ),
    )(*tables, items)


def fetch(items, wanted, columns, column, first_id):
    count, _, rows, width = items.shape
    picks = wanted.shape[1]
    lanes = math.gcd(GROUP, columns)
    planes = columns // lanes
    plane, lane = column // lanes, column % lanes
    part = rows // lanes
    in_plane = [[p * lanes + q for q in range(lanes)] for p in range(planes)]
    in_line = [[p * lanes + q for p in range(planes)] for q in range(lanes)]
    held = lanes * count
    share = -(-count // planes)

    owners = wanted // count
    supplied = jnp.sum((owners.reshape(-1)[:, None] == jnp.arange(columns)[None, :]).astype(jnp.int32), axis=0)
    common = jnp.argmax(supplied).astype(jnp.int32)
    common_plane, common_lane = common // lanes, common % lanes
    is_common = owners == common

    flat = jnp.where(is_common, -1, wanted).reshape(planes, lanes * picks)
    need = jnp.any(flat[:, :, None] == jnp.arange(planes * held)[None, None, :], axis=1)
    need = need.reshape(planes, planes, held).transpose(1, 2, 0)
    foreign = jnp.arange(planes)[:, None] != jnp.arange(planes)[None, :]
    need = need & foreign[:, None, :]
    counted = need.astype(jnp.int32)
    lower = (jnp.arange(held)[:, None] > jnp.arange(held)[None, :]).astype(jnp.int32)
    rank = jnp.sum(lower[None, :, :, None] * counted[:, None, :, :], axis=2)
    totals = jnp.sum(counted, axis=1)
    near = (jnp.arange(planes)[:, None] // 2) == (jnp.arange(planes)[None, :] // 2)
    most = jnp.max(totals - EXTRA * near.astype(jnp.int32))

    mine = lax.dynamic_index_in_dim(counted, plane, 0, keepdims=False)
    my_rank = lax.dynamic_index_in_dim(rank, plane, 0, keepdims=False)
    to_me = lax.dynamic_index_in_dim(rank, plane, 2, keepdims=False)
    asked = lax.dynamic_slice_in_dim(wanted, plane * lanes, lanes, 0)
    asked_plane, asked_item = asked // held, asked % held
    asked_common = (asked // count) == common
    asked_rank = to_me[asked_plane, asked_item]
    shares = jnp.minimum(jnp.arange(planes * share), count - 1).reshape(planes, share)

    def listing(capacity, first=False):
        chosen = mine[:, :, None] * (my_rank[:, :, None] == jnp.arange(capacity)).astype(jnp.int32)
        listed = jnp.sum(chosen * jnp.arange(held)[:, None, None], axis=0)
        parts = [common_lane * count + shares, listed]
        return jnp.concatenate(parts if first else parts[::-1], axis=1)

    def general(capacity):
        def run(items):
            cut = items.reshape(count, 2, lanes, part, width).transpose(2, 0, 1, 3, 4)
            pieces = lax.all_to_all(cut, "node", 0, 0, axis_index_groups=in_plane, tiled=True)
            pieces = pieces.reshape(held, 2, part, width)
            listed = listing(capacity)
            size = capacity + share
            packed = jnp.take(pieces, listed.reshape(-1), axis=0).reshape(planes, size, 2, part, width)
            came = lax.all_to_all(packed, "node", 0, 0, axis_index_groups=in_line, tiled=True)
            own_share = lax.dynamic_index_in_dim(came, common_plane, 0, keepdims=False)[capacity:]
            all_common = lax.all_gather(own_share, "node", axis=0, axis_index_groups=in_line, tiled=True)
            store = jnp.concatenate([pieces, came.reshape(planes * size, 2, part, width), all_common], axis=0)
            at = jnp.where(asked_plane == plane, asked_item, held + asked_plane * size + asked_rank)
            at = jnp.where(asked_common, held + planes * size + asked % count, at)
            outgoing = jnp.take(store, at.reshape(-1), axis=0).reshape(lanes, picks, 2, part, width)
            arrived = lax.all_to_all(outgoing, "node", 0, 0, axis_index_groups=in_plane, tiled=True)
            return arrived.transpose(1, 2, 0, 3, 4).reshape(picks, 2, rows, width)

        return run

    def direct(capacity, collective_id):
        size = capacity + share
        distance = plane ^ asked_plane

        def offset(d):
            return jnp.maximum((d - 1) * size + EXTRA * (d > 1), 0)

        kind = jnp.where(asked_common, 2, jnp.where(distance == 0, 0, 1)).astype(jnp.int32)
        place = jnp.where(distance == 0, asked_item, offset(distance) + share + asked_rank)
        place = jnp.where(asked_common, asked % count, place).astype(jnp.int32)
        away = plane ^ common_plane
        here = common_lane * count + lax.dynamic_index_in_dim(shares, plane, 0, keepdims=False)
        there = offset(away) + jnp.arange(share)
        local = jnp.broadcast_to((away == 0).astype(jnp.int32), (share,))
        hot_table = jnp.stack([here, there, local]).astype(jnp.int32)

        def run(items):
            tables = (listing(capacity + EXTRA, True).astype(jnp.int32), hot_table, kind, place)
            return exchange(lanes, planes, picks, capacity, share, collective_id, tables, items)

        return run

    limit = min(held, lanes * picks)
    steps = [c for c in STEPS if c + EXTRA < limit and planes == 4]
    if not steps:
        return general(limit)(items)
    branch = jnp.sum((most > jnp.array(steps, jnp.int32)).astype(jnp.int32))
    branches = [direct(c, first_id + i) for i, c in enumerate(steps)] + [general(limit)]
    return lax.switch(branch, branches, items)


def per_device(node_blocks, node_slot, pair_list, second_list, targets, spin_signs):
    columns = lax.axis_size("node")
    column = lax.axis_index("node")
    node_col = node_blocks.shape[0]
    pair_col = pair_list.shape[0] // columns
    block_start = column * pair_col
    own_pairs = lax.dynamic_slice_in_dim(pair_list, block_start, pair_col, 0)
    first_slot = node_slot[own_pairs[:, 0]] - column * node_col
    whole_nodes = lax.all_gather(node_blocks, "pair", axis=3, tiled=True)
    first_nodes = jnp.take(whole_nodes, first_slot, axis=0)
    wanted = node_slot[pair_list[:, 1]].reshape(columns, pair_col)
    second_nodes = fetch(node_blocks, wanted, columns, column, 0)
    products = complex_product(first_nodes, second_nodes)
    whole_products = lax.all_gather(products, "pair", axis=3, tiled=True)
    own_seconds = lax.dynamic_slice_in_dim(second_list, block_start, pair_col, 0)
    left_side = jnp.take(whole_products, own_seconds[:, 0] - block_start, axis=0)
    right_side = fetch(products, second_list[:, 1].reshape(columns, pair_col), columns, column, len(STEPS))
    own_signs = lax.dynamic_slice_in_dim(spin_signs, block_start, pair_col, 0).astype(jnp.float32)
    seconds = complex_product(left_side, right_side) * own_signs[:, None, None, None]
    return seconds, column


def solution(mesh):
    placed = (P(("cfg", "node"), None, None, "pair"), P(), P(), P(), P(), P())

    def run(node_blocks, node_slot, pair_list, second_list, targets, spin_signs):
        res_col = RES_COL

        def body(*args):
            seconds, column = per_device(*args)
            pair_col = seconds.shape[0]
            own = lax.dynamic_slice_in_dim(args[4], column * pair_col, pair_col, 0) - column * res_col
            return jnp.stack(
                [
                    jnp.sum(jnp.where((own == r)[:, None, None, None], seconds, 0.0), axis=0)
                    for r in range(res_col)
                ]
            )

        return jax.shard_map(
            body, mesh=mesh, in_specs=placed, out_specs=P(("cfg", "node"), None, None, "pair"), check_vma=False
        )(node_blocks, node_slot, pair_list, second_list, targets, spin_signs)

    return run
```

```python
import functools
import math

import jax
import jax.numpy as jnp
from jax import lax
from jax.experimental import pallas as pl
from jax.experimental.pallas import tpu as pltpu
from jax.sharding import PartitionSpec as P

GROUP = 8
STEPS = (8, 9, 11)
EXTRA = 3
CHUNKS = 4
MESH = pl.DeviceIdType.MESH
RES_COL = 2


def complex_product(left_side, right_side):
    half_width = right_side.shape[3]
    stacked_left = jnp.concatenate([left_side[:, 0], left_side[:, 1]], axis=2)
    real_right = jnp.concatenate([right_side[:, 0], -right_side[:, 1]], axis=1)
    imag_right = jnp.concatenate([right_side[:, 1], right_side[:, 0]], axis=1)
    stacked_right = jnp.concatenate([real_right, imag_right], axis=2)
    joined = jnp.einsum(
        "jmk,jkn->jmn",
        stacked_left,
        stacked_right,
        precision=lax.Precision.HIGH,
        preferred_element_type=jnp.float32,
    )
    return jnp.stack([joined[:, :, :half_width], joined[:, :, half_width:]], axis=1)


def exchange_kernel(
    lanes, planes, count, picks, capacity, share, chunks, ahead,
    send_table, hot_table, kind_table, place_table, items, out, *scratch,
):
    pieces, came, hot = scratch[:chunks], scratch[chunks : 2 * chunks], scratch[2 * chunks : 3 * chunks]
    packed, outgoing, s1, r1, s2, r2, s3, r3, s4, r4, own1, own4 = scratch[3 * chunks :]
    column = lax.axis_index("node")
    plane, lane = column // lanes, column % lanes
    rows = items.shape[2]
    part = rows // lanes
    step = part // chunks
    size = capacity + share

    def beside(e):
        return {"node": plane * lanes + lax.rem(lane + e, lanes)}

    def facing(d):
        low = (plane % 2) * 2
        high = ((plane // 2) % 2) * 4
        return plane + (1 - low if d % 2 else 0) + (2 - high if d >= 2 else 0)

    def along(d):
        return {"node": facing(d) * lanes + lane}

    def size_of(d):
        return size + (EXTRA if d == 1 else 0)

    def offset_of(d):
        return (d - 1) * size + (EXTRA if d > 1 else 0)

    barrier = pltpu.get_barrier_semaphore()
    for e in range(1, lanes):
        pl.semaphore_signal(barrier, inc=1, device_id=beside(e), device_id_type=MESH)
    for d in range(1, planes):
        pl.semaphore_signal(barrier, inc=1, device_id=along(d), device_id_type=MESH)
    pl.semaphore_wait(barrier, lanes - 1 + planes - 1)

    def rows_of(owner, c):
        return pl.ds(pl.multiple_of(owner * part + c * step, step), step)

    first, second, third, last = {}, {}, {}, {}

    def spread(c):
        group = []
        for e in range(1, lanes):
            copy = pltpu.make_async_remote_copy(
                src_ref=items.at[:, :, rows_of(lax.rem(lane + e, lanes), c), :],
                dst_ref=pieces[c].at[pl.ds(lane * count, count)],
                send_sem=s1.at[c, e - 1], recv_sem=r1.at[c, e - 1],
                device_id=beside(e), device_id_type=MESH,
            )
            copy.start()
            group.append(copy)
        copy = pltpu.make_async_copy(
            items.at[:, :, rows_of(lane, c), :], pieces[c].at[pl.ds(lane * count, count)], own1.at[c]
        )
        copy.start()
        first[c] = (group, copy)

    def gathered(c):
        for copy in first[c][0]:
            copy.wait_recv()
        first[c][1].wait()

    def pack(c):
        for d in range(1, planes):
            target = facing(d)

            def move(k, carry, d=d, target=target):
                packed[c, d - 1, k] = pieces[c][send_table[target, k]]
                return carry

            lax.fori_loop(0, size_of(d), move, 0)

    def cross(c):
        second[c] = []
        for d in range(1, planes):
            copy = pltpu.make_async_remote_copy(
                src_ref=packed.at[c, d - 1, pl.ds(0, size_of(d))],
                dst_ref=came[c].at[pl.ds(offset_of(d), size_of(d))],
                send_sem=s2.at[c, d - 1], recv_sem=r2.at[c, d - 1],
                device_id=along(d), device_id_type=MESH,
            )
            copy.start()
            second[c].append(copy)

    def crossed(c):
        for copy in second[c]:
            copy.wait_recv()

    def pass_on(c):
        for i in range(share):
            here = pieces[c][hot_table[0, i]]
            there = came[c][hot_table[1, i]]
            hot[c][plane * share + i] = jnp.where(hot_table[2, i] == 1, here, there)
        third[c] = []
        for d in range(1, planes):
            copy = pltpu.make_async_remote_copy(
                src_ref=hot[c].at[pl.ds(plane * share, share)],
                dst_ref=hot[c].at[pl.ds(plane * share, share)],
                send_sem=s3.at[c, d - 1], recv_sem=r3.at[c, d - 1],
                device_id=along(d), device_id_type=MESH,
            )
            copy.start()
            third[c].append(copy)

    def deliver(c):
        for copy in third[c]:
            copy.wait_recv()
        sent = []
        for e in range(lanes):
            target = lax.rem(lane + e, lanes)

            def move(j, carry, e=e, target=target):
                kind, place = kind_table[target, j], place_table[target, j]
                a = pieces[c][jnp.where(kind == 0, place, 0)]
                b = came[c][jnp.where(kind == 1, place, 0)]
                h = hot[c][jnp.where(kind == 2, place, 0)]
                outgoing[c, e, j] = jnp.where(kind == 0, a, jnp.where(kind == 1, b, h))
                return carry

            lax.fori_loop(0, picks, move, 0)
            if e == 0:
                own = pltpu.make_async_copy(outgoing.at[c, e], out.at[:, :, rows_of(lane, c), :], own4.at[c])
                own.start()
                continue
            copy = pltpu.make_async_remote_copy(
                src_ref=outgoing.at[c, e],
                dst_ref=out.at[:, :, rows_of(lane, c), :],
                send_sem=s4.at[c, e - 1], recv_sem=r4.at[c, e - 1],
                device_id=beside(e), device_id_type=MESH,
            )
            copy.start()
            sent.append(copy)
        last[c] = (sent, own)

    spread(0)
    for c in range(chunks):
        gathered(c)
        if c + 1 < chunks:
            spread(c + 1)
        pack(c)
        if c < ahead:
            cross(c)
    for c in range(chunks):
        crossed(c)
        if c + ahead < chunks:
            cross(c + ahead)
        pass_on(c)
        if c > 0:
            deliver(c - 1)
    deliver(chunks - 1)

    for c in range(chunks):
        for copy in first[c][0] + second[c] + third[c]:
            copy.wait_send()
        for copy in last[c][0]:
            copy.wait()
        last[c][1].wait()


def exchange(lanes, planes, picks, capacity, share, collective_id, tables, items):
    count, _, rows, width = items.shape
    part = rows // lanes
    chunks = CHUNKS if part % (8 * CHUNKS) == 0 else 1
    step = part // chunks
    size = capacity + share
    block = (2, step, width)
    smem = pl.BlockSpec(memory_space=pltpu.SMEM)
    sems = [(chunks, n) for n in (lanes - 1, lanes - 1, planes - 1, planes - 1, planes - 1, planes - 1, lanes - 1, lanes - 1)]
    return pl.pallas_call(
        functools.partial(exchange_kernel, lanes, planes, count, picks, capacity, share, chunks, chunks if count > picks else 2),
        out_shape=jax.ShapeDtypeStruct((picks, 2, rows, width), jnp.float32),
        in_specs=[smem] * 4 + [pl.BlockSpec(memory_space=pl.ANY)],
        out_specs=pl.BlockSpec(memory_space=pl.ANY),
        scratch_shapes=[pltpu.VMEM((lanes * count, *block), jnp.float32)] * chunks
        + [pltpu.VMEM(((planes - 1) * size + EXTRA, *block), jnp.float32)] * chunks
        + [pltpu.VMEM((planes * share, *block), jnp.float32)] * chunks
        + [pltpu.VMEM((chunks, planes - 1, size + EXTRA, *block), jnp.float32)]
        + [pltpu.VMEM((chunks, lanes, picks, *block), jnp.float32)]
        + [pltpu.SemaphoreType.DMA(s) for s in sems]
        + [pltpu.SemaphoreType.DMA((chunks,))] * 2,
        compiler_params=pltpu.CompilerParams(
            collective_id=collective_id, has_side_effects=True, vmem_limit_bytes=40 * 2**20
        ),
    )(*tables, items)


def fetch(items, wanted, columns, column, first_id):
    count, _, rows, width = items.shape
    picks = wanted.shape[1]
    lanes = math.gcd(GROUP, columns)
    planes = columns // lanes
    plane, lane = column // lanes, column % lanes
    part = rows // lanes
    in_plane = [[p * lanes + q for q in range(lanes)] for p in range(planes)]
    in_line = [[p * lanes + q for p in range(planes)] for q in range(lanes)]
    held = lanes * count
    share = -(-count // planes)

    owners = wanted // count
    supplied = jnp.sum((owners.reshape(-1)[:, None] == jnp.arange(columns)[None, :]).astype(jnp.int32), axis=0)
    common = jnp.argmax(supplied).astype(jnp.int32)
    common_plane, common_lane = common // lanes, common % lanes
    is_common = owners == common

    flat = jnp.where(is_common, -1, wanted).reshape(planes, lanes * picks)
    need = jnp.any(flat[:, :, None] == jnp.arange(planes * held)[None, None, :], axis=1)
    need = need.reshape(planes, planes, held).transpose(1, 2, 0)
    foreign = jnp.arange(planes)[:, None] != jnp.arange(planes)[None, :]
    need = need & foreign[:, None, :]
    counted = need.astype(jnp.int32)
    lower = (jnp.arange(held)[:, None] > jnp.arange(held)[None, :]).astype(jnp.int32)
    rank = jnp.sum(lower[None, :, :, None] * counted[:, None, :, :], axis=2)
    totals = jnp.sum(counted, axis=1)
    near = (jnp.arange(planes)[:, None] // 2) == (jnp.arange(planes)[None, :] // 2)
    most = jnp.max(totals - EXTRA * near.astype(jnp.int32))

    mine = lax.dynamic_index_in_dim(counted, plane, 0, keepdims=False)
    my_rank = lax.dynamic_index_in_dim(rank, plane, 0, keepdims=False)
    to_me = lax.dynamic_index_in_dim(rank, plane, 2, keepdims=False)
    asked = lax.dynamic_slice_in_dim(wanted, plane * lanes, lanes, 0)
    asked_plane, asked_item = asked // held, asked % held
    asked_common = (asked // count) == common
    asked_rank = to_me[asked_plane, asked_item]
    shares = jnp.minimum(jnp.arange(planes * share), count - 1).reshape(planes, share)

    def listing(capacity, first=False):
        chosen = mine[:, :, None] * (my_rank[:, :, None] == jnp.arange(capacity)).astype(jnp.int32)
        listed = jnp.sum(chosen * jnp.arange(held)[:, None, None], axis=0)
        parts = [common_lane * count + shares, listed]
        return jnp.concatenate(parts if first else parts[::-1], axis=1)

    def general(capacity):
        def run(items):
            cut = items.reshape(count, 2, lanes, part, width).transpose(2, 0, 1, 3, 4)
            pieces = lax.all_to_all(cut, "node", 0, 0, axis_index_groups=in_plane, tiled=True)
            pieces = pieces.reshape(held, 2, part, width)
            listed = listing(capacity)
            size = capacity + share
            packed = jnp.take(pieces, listed.reshape(-1), axis=0).reshape(planes, size, 2, part, width)
            came = lax.all_to_all(packed, "node", 0, 0, axis_index_groups=in_line, tiled=True)
            own_share = lax.dynamic_index_in_dim(came, common_plane, 0, keepdims=False)[capacity:]
            all_common = lax.all_gather(own_share, "node", axis=0, axis_index_groups=in_line, tiled=True)
            store = jnp.concatenate([pieces, came.reshape(planes * size, 2, part, width), all_common], axis=0)
            at = jnp.where(asked_plane == plane, asked_item, held + asked_plane * size + asked_rank)
            at = jnp.where(asked_common, held + planes * size + asked % count, at)
            outgoing = jnp.take(store, at.reshape(-1), axis=0).reshape(lanes, picks, 2, part, width)
            arrived = lax.all_to_all(outgoing, "node", 0, 0, axis_index_groups=in_plane, tiled=True)
            return arrived.transpose(1, 2, 0, 3, 4).reshape(picks, 2, rows, width)

        return run

    def direct(capacity, collective_id):
        size = capacity + share
        distance = plane ^ asked_plane

        def offset(d):
            return jnp.maximum((d - 1) * size + EXTRA * (d > 1), 0)

        kind = jnp.where(asked_common, 2, jnp.where(distance == 0, 0, 1)).astype(jnp.int32)
        place = jnp.where(distance == 0, asked_item, offset(distance) + share + asked_rank)
        place = jnp.where(asked_common, asked % count, place).astype(jnp.int32)
        away = plane ^ common_plane
        here = common_lane * count + lax.dynamic_index_in_dim(shares, plane, 0, keepdims=False)
        there = offset(away) + jnp.arange(share)
        local = jnp.broadcast_to((away == 0).astype(jnp.int32), (share,))
        hot_table = jnp.stack([here, there, local]).astype(jnp.int32)

        def run(items):
            tables = (listing(capacity + EXTRA, True).astype(jnp.int32), hot_table, kind, place)
            return exchange(lanes, planes, picks, capacity, share, collective_id, tables, items)

        return run

    limit = min(held, lanes * picks)
    steps = [c for c in STEPS if c + EXTRA < limit and planes == 4]
    if not steps:
        return general(limit)(items)
    branch = jnp.sum((most > jnp.array(steps, jnp.int32)).astype(jnp.int32))
    branches = [direct(c, first_id + i) for i, c in enumerate(steps)] + [general(limit)]
    return lax.switch(branch, branches, items)


def per_device(node_blocks, node_slot, pair_list, second_list, targets, spin_signs):
    columns = lax.axis_size("node")
    column = lax.axis_index("node")
    node_col = node_blocks.shape[0]
    pair_col = pair_list.shape[0] // columns
    block_start = column * pair_col
    own_pairs = lax.dynamic_slice_in_dim(pair_list, block_start, pair_col, 0)
    first_slot = node_slot[own_pairs[:, 0]] - column * node_col
    whole_nodes = lax.all_gather(node_blocks, "pair", axis=3, tiled=True)
    first_nodes = jnp.take(whole_nodes, first_slot, axis=0)
    wanted = node_slot[pair_list[:, 1]].reshape(columns, pair_col)
    second_nodes = fetch(node_blocks, wanted, columns, column, 0)
    products = complex_product(first_nodes, second_nodes)
    whole_products = lax.all_gather(products, "pair", axis=3, tiled=True)
    own_seconds = lax.dynamic_slice_in_dim(second_list, block_start, pair_col, 0)
    left_side = jnp.take(whole_products, own_seconds[:, 0] - block_start, axis=0)
    right_side = fetch(products, second_list[:, 1].reshape(columns, pair_col), columns, column, len(STEPS))
    own_signs = lax.dynamic_slice_in_dim(spin_signs, block_start, pair_col, 0).astype(jnp.float32)
    seconds = complex_product(left_side, right_side) * own_signs[:, None, None, None]
    return seconds, column


def solution(mesh):
    placed = (P(("cfg", "node"), None, None, "pair"), P(), P(), P(), P(), P())

    def run(node_blocks, node_slot, pair_list, second_list, targets, spin_signs):
        res_col = RES_COL

        def body(*args):
            seconds, column = per_device(*args)
            pair_col = seconds.shape[0]
            own = lax.dynamic_slice_in_dim(args[4], column * pair_col, pair_col, 0) - column * res_col
            return jnp.stack(
                [
                    jnp.sum(jnp.where((own == r)[:, None, None, None], seconds, 0.0), axis=0)
                    for r in range(res_col)
                ]
            )

        return jax.shard_map(
            body, mesh=mesh, in_specs=placed, out_specs=P(("cfg", "node"), None, None, "pair"), check_vma=False
        )(node_blocks, node_slot, pair_list, second_list, targets, spin_signs)

    return run
```
